32 devices in a mesh: parts: 2 (over x), user: 16 (over z, y, core).
Axes of the slice: x: 2, y: 2, z: 4, core: 2. Of those that a mesh axis runs over, the one named last changes fastest.
Arguments:
- user_factors: float32 [32768, 64], P(('parts', 'user')), parts along dimension 0, may hold values from -2 to 2
- item_factors: float32 [16384, 64], P(('parts', 'user')), parts along dimension 0, may hold values from -2 to 2
- ratings: bfloat16 [32, 64, 256, 256], P(('parts', 'user')), parts along dimension 0, may hold values from -6 to 6
- rating_len: int32 [32, 64, 256], P(('parts', 'user')), parts along dimension 0, may hold values from 0 to 256, as said below
- rating_user: int32 [32, 64], P(('parts', 'user')), parts along dimension 0, may hold values from 0 to 3
- rating_item: int32 [32, 64], P(('parts', 'user')), parts along dimension 0, may hold values from 0 to 31
- trust_src: int32 [32, 16, 3], P(('parts', 'user')), parts along dimension 0, may hold values from 0 to 3
- trust_dst: int32 [32, 16, 3], P(('parts', 'user')), parts along dimension 0, may hold values from 0 to 3
- trust_weight: bfloat16 [32, 16, 3, 256, 256], P(('parts', 'user')), parts along dimension 0, may hold values from 0 to 1
Outputs:
- user_grad: float32 [32768, 64], P(('parts', 'user')), parts along dimension 0
- item_grad: float32 [16384, 64], P(('parts', 'user')), parts along dimension 0
The draws below stay inside these ranges and needn't reach their ends.
There are 2 independent parts, one for each index of `parts`. The reference program is written for one: setup_inputs(seed, part) draws one part's arguments, and reference() takes and returns one part's arrays. A program takes and returns all parts, laid end to end along the dimension named above; each array names one. Nothing has to cross between parts.
Inputs may be any that keep to these rules, and one draw needn't show every extreme that they name: rating_len[d, r, a] counts the leading item columns of tile r rated by row a; in every tile some row has all 256 and some has none.
All inputs are finite; a program needn't handle non-finite values.
Results may differ from the reference program's by a relative error of at most 0.0031.
Values may be sent and summed in bfloat16 or wider, within the bound.
A program may use at most 128 MiB of HBM per device.

```python
import jax
import jax.numpy as jnp
from jax import lax

K = 64
BLOCK = 256
UB_DEV = 4
R_DEV = 64
CAP = 3
PEERS = 16
USERS = 16384
ITEMS = 8192
ITEM_BLOCKS = 32
N_USER = 16


def draw_rating_len(key, part):
    key = jax.random.fold_in(key, 11)
    counts = jax.random.randint(key, (PEERS, R_DEV, BLOCK), 0, BLOCK + 1)
    counts = counts.at[:, :, 0].set(BLOCK)
    counts = counts.at[:, :, 1].set(0)
    return counts.astype(jnp.int32)


def draw_trust_weight(key, part):
    key = jax.random.fold_in(key, 23)
    key_rate, key_link, key_value = jax.random.split(key, 3)
    shape = (PEERS, PEERS, CAP, BLOCK, BLOCK)
    rate = jnp.exp(jax.random.uniform(key_rate, (PEERS, PEERS, CAP, BLOCK, 1), jnp.float32, jnp.log(0.25), jnp.log(8.0))) / BLOCK
    linked = (jax.random.uniform(key_link, shape, jnp.float32) < rate).astype(jnp.float32)
    strength = jax.random.uniform(key_value, shape, jnp.float32, 0.2, 1.0)
    return (strength * linked).astype(jnp.bfloat16)


def set_ends(drawn, own_key, least, top_value):
    longest = drawn.shape.index(max(drawn.shape))
    spots = []
    for shift in (0, 1):
        where = [jax.random.randint(jax.random.fold_in(own_key, axis), (), 0, length) for axis, length in enumerate(drawn.shape)]
        where[longest] = (where[longest] + shift) % drawn.shape[longest]
        spots.append(tuple(where))
    return drawn.at[spots[0]].set(least).at[spots[1]].set(top_value)


def shard_levels(rng, dims, cuts, low, largest):
    gain = 1.0
    for dim, shards_of in cuts:
        heights = jax.random.uniform(jax.random.fold_in(jax.random.fold_in(rng, 6), dim), (shards_of,), jnp.float32, low / len(cuts), largest / len(cuts))
        gain = gain * jnp.repeat(jnp.exp(heights), dims[dim] // shards_of).reshape((-1,) + (1,) * (len(dims) - 1 - dim))
    return gain


def bell_draw(key, extent, spread, limit, cuts=(), kind=jnp.bfloat16):
    array = jax.random.normal(key, extent, jnp.float32) * spread
    if len(cuts) > 0:
        array = shard_levels(key, extent, cuts, -0.22, 0.18) * array
    return jnp.clip(array, min=-limit, max=limit).astype(kind)


def setup_inputs(seed: int = 0, part: int = 0) -> dict:
    key_list = jax.random.split(jax.random.key(seed), 10)
    part_splits = jax.random.split(jax.random.fold_in(key_list[9], part), 10)
    return {
        "user_factors": bell_draw(part_splits[0], (USERS, K), 0.35, 2.0, ((0, 16),), jnp.float32),
        "item_factors": bell_draw(part_splits[1], (ITEMS, K), 0.35, 2.0, ((0, 16),), jnp.float32),
        "ratings": bell_draw(part_splits[2], (PEERS, R_DEV, BLOCK, BLOCK), 1.0, 6.0, ((0, 16),)),
        "rating_len": draw_rating_len(jax.random.fold_in(jax.random.fold_in(key_list[9], part), 71), part),
        "rating_user": set_ends(jax.random.randint(part_splits[4], (PEERS, R_DEV), 0, UB_DEV), jax.random.fold_in(part_splits[4], 1), 0, UB_DEV - 1).astype(jnp.int32),
        "rating_item": set_ends(jax.random.randint(part_splits[5], (PEERS, R_DEV), 0, ITEM_BLOCKS), jax.random.fold_in(part_splits[5], 1), 0, ITEM_BLOCKS - 1).astype(jnp.int32),
        "trust_src": set_ends(jax.random.randint(part_splits[6], (PEERS, PEERS, CAP), 0, UB_DEV), jax.random.fold_in(part_splits[6], 1), 0, UB_DEV - 1).astype(jnp.int32),
        "trust_dst": set_ends(jax.random.randint(part_splits[7], (PEERS, PEERS, CAP), 0, UB_DEV), jax.random.fold_in(part_splits[7], 1), 0, UB_DEV - 1).astype(jnp.int32),
        "trust_weight": draw_trust_weight(jax.random.fold_in(jax.random.fold_in(key_list[9], part), 71), part),
    }


reg_coef = 0.05
social_coef = 8.0


def reference(user_factors, item_factors, ratings, rating_len, rating_user, rating_item, trust_src, trust_dst, trust_weight):
    width = user_factors.shape[1]
    user_blocks = user_factors.reshape(-1, BLOCK, width)
    user_half = lax.optimization_barrier(user_blocks.astype(jnp.bfloat16)).astype(jnp.float32)
    item_half = lax.optimization_barrier(item_factors.astype(jnp.bfloat16)).astype(jnp.float32).reshape(-1, BLOCK, width)
    peer_ids = jnp.arange(N_USER, dtype=jnp.int32)
    local_ids = jnp.arange(UB_DEV, dtype=jnp.int32)
    columns = jnp.arange(BLOCK, dtype=jnp.int32)

    def visit(carry, inputs):
        user_acc, item_acc, returned = carry
        device, tile_ratings, tile_lengths, tile_users, tile_items, truster_ids, trustee_ids, weights = inputs
        user_rows = user_half[device * UB_DEV + tile_users]
        item_rows = item_half[tile_items]
        predicted = jnp.einsum("rak,rbk->rab", user_rows, item_rows)
        rated = columns[None, None, :] < tile_lengths[:, :, None]
        errors = jnp.where(rated, predicted - tile_ratings.astype(jnp.float32), 0.0).astype(jnp.bfloat16)
        errors = lax.optimization_barrier(errors).astype(jnp.float32)
        user_terms = jnp.einsum("rab,rbk->rak", errors, item_rows)
        choose = (tile_users[:, None] == local_ids[None, :]).astype(jnp.float32)
        own_terms = jnp.einsum("rc,rak->cak", choose, user_terms)
        item_terms = jnp.einsum("rab,rak->rbk", errors, user_rows)
        item_acc = item_acc.at[tile_items].add(item_terms)
        trustee_global = peer_ids[:, None] * UB_DEV + trustee_ids
        fetched = user_half[trustee_global]
        weight_full = weights.astype(jnp.float32)
        tile_sums = jnp.sum(weight_full, axis=-1)
        pick = (truster_ids[:, :, None] == local_ids[None, None, :]).astype(jnp.float32)
        denominator = 1.0 + jnp.einsum("pcu,pca->ua", pick, tile_sums)
        pulled = jnp.einsum("pcab,pcbk->pcak", weight_full, fetched)
        collected = jnp.einsum("pcu,pcak->uak", pick, pulled)
        mine = lax.dynamic_slice_in_dim(user_blocks, device * UB_DEV, UB_DEV, 0)
        pull_error = mine - collected / denominator[:, :, None]
        scaled = (pull_error / denominator[:, :, None]).astype(jnp.bfloat16)
        scaled = lax.optimization_barrier(scaled).astype(jnp.float32)
        per_tile = scaled[truster_ids]
        contrib = jnp.einsum("pcab,pcak->pcbk", weight_full, per_tile)
        returned = returned.at[trustee_global].add(contrib)
        user_acc = lax.dynamic_update_slice_in_dim(user_acc, own_terms + social_coef * pull_error, device * UB_DEV, 0)
        return (user_acc, item_acc, returned), None

    start = (jnp.zeros(user_blocks.shape, jnp.float32), jnp.zeros(item_half.shape, jnp.float32), jnp.zeros(user_blocks.shape, jnp.float32))
    inputs = (peer_ids, ratings, rating_len, rating_user, rating_item, trust_src, trust_dst, trust_weight)
    (user_acc, item_acc, returned), unused = lax.scan(visit, start, inputs)
    user_grad = user_acc - social_coef * returned + reg_coef * user_blocks
    item_grad = item_acc.reshape(-1, width) + reg_coef * item_factors
    return user_grad.reshape(-1, width), item_grad
```

```python
import functools

import jax
import jax.numpy as jnp
from jax import lax
from jax.experimental import pallas as pl
from jax.experimental.pallas import tpu as pltpu
from jax.sharding import PartitionSpec as P

reg_coef = 0.05
social_coef = 8.0
GROUP = 4
NT = (((1,), (1,)), ((), ()))
F32 = jnp.float32
BF16 = jnp.bfloat16


def kernel(
    n, uf_ref, if_ref, rat_hbm, len_ref, ruser, ritem, tsrc, tdst, w_hbm, links,
    ug_ref, ig_ref,
    rat, w, gi, gu, unat, utf, itf, uto, lens, run, uacc, pacc, pe, scaled,
    ci, ric, riy, riu, rid, cu, ruc, ruy, ruu, rud, own_i, own_u,
    load_sem, agi_s, agi_r, agu_s, agu_r,
    ici_s, ici_r, iy_s, iy_r, iz_s, iz_r,
    uci_s, uci_r, uy_s, uy_r, uz_s, uz_r,
):
    me = lax.axis_index("user")
    H = n // 4
    z = me // 4
    y = (me // 2) % 2
    c = me % 2
    oc = 1 - c
    oy = 1 - y
    T = uf_ref.shape[0] // unat.shape[0]
    K = uf_ref.shape[1]
    ub = unat.shape[0]
    ib = if_ref.shape[0] // T
    R = rat.shape[0]
    cap = w.shape[0] // n

    def at(zz, yy, cc):
        return zz * 4 + yy * 2 + cc

    core = at(z, y, oc)
    side = at(z, oy, c)
    up = at(z + 1, y, c)
    down = at(z - 1, y, c)
    has_up = z < H - 1
    has_down = z > 0

    def remote(src, dst, s, r, dev):
        return pltpu.make_async_remote_copy(
            src_ref=src, dst_ref=dst, send_sem=s, recv_sem=r,
            device_id={"user": dev}, device_id_type=pl.DeviceIdType.MESH,
        )

    loads = []
    parts = 4
    for q in range(parts):
        rows = pl.ds(q * (R // parts), R // parts)
        loads.append(pltpu.make_async_copy(rat_hbm.at[0, rows], rat.at[rows], load_sem.at[q]))
    for q in range(parts):
        rows = pl.ds(q * (n // parts), n // parts)
        wide = pl.ds(q * (n * cap // parts), n * cap // parts)
        loads.append(pltpu.make_async_copy(w_hbm.at[wide], w.at[wide], load_sem.at[parts + q]))

    for b in range(ib):
        t = jnp.transpose(if_ref[pl.ds(b * T, T), :])
        itf[pl.ds(b * K, K), :] = t
        gi[me * ib + b] = t.astype(BF16)

    barrier = pltpu.get_barrier_semaphore()

    def greet(dev):
        pl.semaphore_signal(barrier, inc=1, device_id={"user": dev}, device_id_type=pl.DeviceIdType.MESH)

    greet(core)
    greet(side)

    @pl.when(has_up)
    def _():
        greet(up)

    @pl.when(has_down)
    def _():
        greet(down)

    pl.semaphore_wait(barrier, 2 + has_up.astype(jnp.int32) + has_down.astype(jnp.int32))

    class Gather:
        def __init__(self, buf, width, s, r):
            self.buf, self.width, self.s, self.r = buf, width, s, r

        def copy(self, o, way, dev):
            part = self.buf.at[pl.ds(o * self.width, self.width)]
            return remote(part, part, self.s.at[way, o], self.r.at[o], dev)

        def first(self):
            @pl.when(has_up)
            def _():
                self.copy(me, 0, up).start()

            @pl.when(has_down)
            def _():
                self.copy(me, 1, down).start()

            self.copy(me, 2, side).start()
            self.copy(me, 3, core).start()

        def from_side(self, zz):
            o = at(zz, oy, c)
            self.copy(o, 3, side).wait_recv()
            self.copy(o, 3, core).start()

        def step(self, t):
            @pl.when(z - t >= 0)
            def _():
                o = at(z - t, y, c)
                self.copy(o, 0, core).wait_recv()

                @pl.when(has_up)
                def _():
                    self.copy(o, 0, up).start()

                self.copy(o, 2, side).start()
                self.copy(o, 3, core).start()

            @pl.when(z + t < H)
            def _():
                o = at(z + t, y, c)
                self.copy(o, 1, core).wait_recv()

                @pl.when(has_down)
                def _():
                    self.copy(o, 1, down).start()

                self.copy(o, 2, side).start()
                self.copy(o, 3, core).start()

            self.late(t - 1)

        def late(self, t):
            @pl.when(z - t >= 0)
            def _():
                self.from_side(z - t)

            @pl.when(jnp.logical_and(z + t < H, t > 0))
            def _():
                self.from_side(z + t)

        def finish(self):
            self.late(H - 1)

            def arrive(k, _):
                o = at(k // 2, k % 2, oc)
                self.copy(o, 3, core).wait_recv()
                return 0

            lax.fori_loop(0, n // 2, arrive, 0)

        def drain(self):
            def sent(k, _):
                o = at(k, y, c)

                @pl.when(jnp.logical_and(has_up, k <= z))
                def _():
                    self.copy(o, 0, up).wait_send()

                @pl.when(jnp.logical_and(has_down, k >= z))
                def _():
                    self.copy(o, 1, down).wait_send()

                self.copy(o, 2, side).wait_send()
                self.copy(o, 3, core).wait_send()
                self.copy(at(k, oy, c), 3, core).wait_send()
                return 0

            lax.fori_loop(0, H, sent, 0)

    items = Gather(gi, ib, agi_s, agi_r)
    users = Gather(gu, ub, agu_s, agu_r)
    items.first()
    for load in loads:
        load.start()

    zero = jnp.zeros((K, T), BF16)
    for b in range(ub):
        x = uf_ref[pl.ds(b * T, T), :]
        t = jnp.transpose(x)
        utf[pl.ds(b * K, K), :] = t
        t = t.astype(BF16)
        gu[me * ub + b] = t
        uto[b] = t
        unat[b] = x.astype(BF16)
    gi[n * ib] = zero
    scaled[ub] = zero
    items.step(1)
    users.first()
    lent = jnp.transpose(len_ref[0].astype(F32))
    for g in range(R // GROUP):
        lens[g] = lent[:, g * GROUP:(g + 1) * GROUP]
    run[0] = jnp.zeros((K, T), F32)
    uacc[...] = jnp.zeros(uacc.shape, F32)
    pacc[...] = jnp.zeros(pacc.shape, F32)
    for t in range(2, H):
        items.step(t)
    items.finish()
    for load in loads[:parts]:
        load.wait()

    columns = lax.broadcasted_iota(jnp.int32, (T, T), 1).astype(F32)
    every = (R // GROUP) // H

    def rate(g, _):
        @pl.when(jnp.logical_and(g % every == 0, g // every + 1 < H))
        def _():
            users.step(g // every + 1)

        cut = lens[g]
        errs = []
        picks = []
        for j in range(GROUP):
            r = g * GROUP + j
            u = ruser[0, r]
            i = ritem[0, r]
            pred = jnp.dot(unat[u], gi[i], preferred_element_type=F32)
            e = jnp.where(columns < cut[:, j:j + 1], pred - rat[r].astype(F32), 0.0).astype(BF16)
            errs.append(e)
            picks.append(jnp.concatenate(
                [gi[jnp.where(u == b, i, n * ib)] for b in range(ub)], axis=0))
            term = jnp.dot(uto[u], e, preferred_element_type=F32)
            run[r + 1] = term + run[links[r]]
        uacc[...] += lax.dot_general(
            jnp.concatenate(picks, axis=1), jnp.concatenate(errs, axis=1), NT,
            preferred_element_type=F32)
        return 0

    lax.fori_loop(0, R // GROUP, rate, 0)

    class Reduce:
        def __init__(self, buf, width, rc, ry, ru, rd, own, cs, cr, ys, yr, zs, zr):
            self.buf, self.width, self.own = buf, width, own
            self.rc, self.ry, self.ru, self.rd = rc, ry, ru, rd
            self.cs, self.cr, self.ys, self.yr, self.zs, self.zr = cs, cr, ys, yr, zs, zr

        def cross(self, zz, yy):
            k = zz * 2 + yy
            return remote(self.buf.at[at(zz, yy, oc)], self.rc.at[k], self.cs.at[k], self.cr.at[k], core)

        def aside(self, zz):
            return remote(self.buf.at[at(zz, oy, c)], self.ry.at[zz], self.ys.at[zz], self.yr.at[zz], side)

        def climb(self, zz):
            return remote(self.buf.at[at(zz, y, c)], self.ru.at[zz], self.zs.at[zz], self.zr.at[0, zz], up)

        def sink(self, zz):
            return remote(self.buf.at[at(zz, y, c)], self.rd.at[zz], self.zs.at[zz], self.zr.at[1, zz], down)

        def turn(self, zz):
            self.cross(zz, oy).wait_recv()
            d = at(zz, oy, c)
            self.buf[d] = (self.buf[d].astype(F32) + self.rc[zz * 2 + oy].astype(F32)).astype(BF16)
            self.aside(zz).start()

        def line(self, zz):
            d = at(zz, y, c)
            self.cross(zz, y).wait_recv()
            self.aside(zz).wait_recv()
            self.own[...] = (self.buf[d].astype(F32) + self.rc[zz * 2 + y].astype(F32)
                             + self.ry[zz].astype(F32))

            @pl.when(jnp.logical_and(z <= zz, has_down))
            def _():
                self.climb(zz).wait_recv()
                self.own[...] += self.ru[zz].astype(F32)

            @pl.when(jnp.logical_and(z >= zz, has_up))
            def _():
                self.sink(zz).wait_recv()
                self.own[...] += self.rd[zz].astype(F32)

            @pl.when(z != zz)
            def _():
                self.buf[d] = self.own[...].astype(BF16)

            @pl.when(z < zz)
            def _():
                self.climb(zz).start()

            @pl.when(z > zz)
            def _():
                self.sink(zz).start()

            @pl.when(z == zz)
            def _():
                self.buf_own[...] = self.own[...]

        def drain(self):
            def sent(k, _):
                self.cross(k, 0).wait_send()
                self.cross(k, 1).wait_send()
                self.aside(k).wait_send()

                @pl.when(z < k)
                def _():
                    self.climb(k).wait_send()

                @pl.when(z > k)
                def _():
                    self.sink(k).wait_send()

                return 0

            lax.fori_loop(0, H, sent, 0)

    item_sum = Reduce(ci, ib, ric, riy, riu, rid, own_i.at[0], ici_s, ici_r, iy_s, iy_r, iz_s, iz_r)
    item_sum.buf_own = own_i.at[1]
    user_sum = Reduce(cu, ub, ruc, ruy, ruu, rud, own_u.at[0], uci_s, uci_r, uy_s, uy_r, uz_s, uz_r)
    user_sum.buf_own = own_u.at[1]

    def order(k):
        odd = k % 2
        return (1 - odd) * (H - 1 - k // 2) + odd * (k // 2)

    def fill(d):
        for b in range(ib):
            ci[d, pl.ds(b * K, K), :] = run[links[R + d * ib + b]].astype(BF16)

    def fill_other(k, _):
        for yy in (oy, y):
            fill(at(order(k), yy, oc))
            item_sum.cross(order(k), yy).start()
        return 0

    def fill_mine(k, _):
        for yy in (oy, y):
            fill(at(order(k), yy, c))
        return 0

    lax.fori_loop(0, H, fill_other, 0)
    lax.fori_loop(0, H, fill_mine, 0)
    users.finish()
    gu[n * ub] = zero
    for load in loads[parts:]:
        load.wait()

    row = lax.broadcasted_iota(jnp.int32, (16, T), 0)

    def pull(p, _):
        @pl.when(jnp.logical_and(p >= n - H, p < n))
        def _():
            item_sum.turn(order(p - (n - H)))

        lhs = []
        rhs = []
        for k in range(cap):
            s = tsrc[0, p, k]
            t = p * ub + tdst[0, p, k]
            ones = jnp.where(row == s, 1.0, 0.0).astype(BF16)
            lhs.append(jnp.concatenate(
                [gu[jnp.where(s == b, t, n * ub)] for b in range(ub)] + [ones], axis=0))
            rhs.append(w[p * cap + k])
        pacc[...] += lax.dot_general(
            jnp.concatenate(lhs, axis=1), jnp.concatenate(rhs, axis=1), NT,
            preferred_element_type=F32)
        return 0

    lax.fori_loop(0, n, pull, 0)
    for b in range(ub):
        den = 1.0 + pacc[ub * K + b:ub * K + b + 1, :]
        rows = pl.ds(b * K, K)
        err = utf[rows, :] - pacc[rows, :] / den
        pe[rows, :] = err
        scaled[b] = (err / den).astype(BF16)

    def give(p):
        lhs = []
        for k in range(cap):
            s = tsrc[0, p, k]
            t = tdst[0, p, k]
            lhs.append(jnp.concatenate(
                [scaled[jnp.where(t == b, s, ub)] for b in range(ub)], axis=0))
        tiles = w[pl.ds(p * cap, cap)].reshape(cap * T, T)
        cu[p] = jnp.dot(jnp.concatenate(lhs, axis=1), tiles, preferred_element_type=F32).astype(BF16)

    def give_other(k, _):
        zz = order(k % H)
        yy = (k // H) * y + (1 - k // H) * oy
        give(at(zz, yy, oc))
        user_sum.cross(zz, yy).start()
        return 0

    def give_side(k, _):
        zz = order(k)
        give(at(zz, oy, c))
        user_sum.turn(zz)
        return 0

    def give_mine(k, _):
        give(at(order(k), y, c))
        item_sum.line(order(k))
        return 0

    def user_line(k, _):
        user_sum.line(order(k))
        return 0

    lax.fori_loop(0, 2 * H, give_other, 0)
    lax.fori_loop(0, H, give_side, 0)
    lax.fori_loop(0, H, give_mine, 0)
    for b in range(ib):
        rows = pl.ds(b * K, K)
        ig_ref[pl.ds(b * T, T), :] = jnp.transpose(own_i[1, rows, :] + reg_coef * itf[rows, :])
    lax.fori_loop(0, H, user_line, 0)
    for b in range(ub):
        rows = pl.ds(b * K, K)
        total = (uacc[rows, :] + social_coef * (pe[rows, :] - own_u[1, rows, :])
                 + reg_coef * utf[rows, :])
        ug_ref[pl.ds(b * T, T), :] = jnp.transpose(total)
    items.drain()
    users.drain()
    item_sum.drain()
    user_sum.drain()


def body(n, user_factors, item_factors, ratings, rating_len, rating_user, rating_item,
         trust_src, trust_dst, trust_weight):
    T = ratings.shape[-1]
    K = user_factors.shape[1]
    ub = user_factors.shape[0] // T
    ib = item_factors.shape[0] // T
    R = ratings.shape[1]
    cap = trust_src.shape[2]
    H = n // 4
    tile_items = rating_item[0]
    ids = jnp.concatenate([tile_items, jnp.arange(n * ib, dtype=jnp.int32)])
    limit = jnp.minimum(jnp.arange(R + n * ib, dtype=jnp.int32), R)
    at = jnp.arange(R, dtype=jnp.int32)
    links = jnp.max(jnp.where((ids[:, None] == tile_items[None, :]) & (at[None, :] < limit[:, None]),
                              at[None, :] + 1, 0), axis=1)
    weights = trust_weight.reshape(n * cap, T, T)
    vmem = pl.BlockSpec(memory_space=pltpu.VMEM)
    smem = pl.BlockSpec(memory_space=pltpu.SMEM)
    hbm = pl.BlockSpec(memory_space=pl.ANY)
    dma = pltpu.SemaphoreType.DMA
    scratch = [
        pltpu.VMEM((R, T, T), BF16),
        pltpu.VMEM((n * cap, T, T), BF16),
        pltpu.VMEM((n * ib + 1, K, T), BF16),
        pltpu.VMEM((n * ub + 1, K, T), BF16),
        pltpu.VMEM((ub, T, K), BF16),
        pltpu.VMEM((ub * K, T), F32),
        pltpu.VMEM((ib * K, T), F32),
        pltpu.VMEM((ub, K, T), BF16),
        pltpu.VMEM((R // GROUP, T, GROUP), F32),
        pltpu.VMEM((R + 1, K, T), F32),
        pltpu.VMEM((ub * K, T), F32),
        pltpu.VMEM((ub * K + 16, T), F32),
        pltpu.VMEM((ub * K, T), F32),
        pltpu.VMEM((ub + 1, K, T), BF16),
    ]
    for width in (ib, ub):
        scratch += [pltpu.VMEM((count, width * K, T), BF16) for count in (n, n // 2, H, H, H)]
    scratch += [pltpu.VMEM((2, width * K, T), F32) for width in (ib, ub)]
    scratch += [dma((8,)), dma((4, n)), dma((n,)), dma((4, n)), dma((n,))]
    for _ in range(2):
        scratch += [dma((n // 2,)), dma((n // 2,)), dma((H,)), dma((H,)), dma((H,)), dma((2, H))]
    return pl.pallas_call(
        functools.partial(kernel, n),
        out_shape=(jax.ShapeDtypeStruct(user_factors.shape, F32),
                   jax.ShapeDtypeStruct(item_factors.shape, F32)),
        in_specs=[vmem, vmem, hbm, vmem, smem, smem, smem, smem, hbm, smem],
        out_specs=(vmem, vmem),
        scratch_shapes=scratch,
        compiler_params=pltpu.CompilerParams(
            collective_id=0, has_side_effects=True, vmem_limit_bytes=56 * 1024 * 1024),
    )(user_factors, item_factors, ratings, rating_len, rating_user, rating_item,
      trust_src, trust_dst, weights, links)


def solution(mesh):
    row = P(("parts", "user"))
    return jax.shard_map(
        functools.partial(body, mesh.shape["user"]), mesh=mesh,
        in_specs=(row,) * 9, out_specs=(row, row), check_vma=False)
```

```python
import functools

import jax
import jax.numpy as jnp
from jax import lax
from jax.experimental import pallas as pl
from jax.experimental.pallas import tpu as pltpu
from jax.sharding import PartitionSpec as P

reg_coef = 0.05
social_coef = 8.0
GROUP = 4
NT = (((1,), (1,)), ((), ()))
F32 = jnp.float32
BF16 = jnp.bfloat16


def kernel(
    n, uf_ref, if_ref, rat_hbm, len_ref, ruser, ritem, tsrc, tdst, w_hbm, links,
    ug_ref, ig_ref,
    rat, w, gi, gu, unat, utf, itf, uto, lens, run, uacc, pacc, pe, scaled,
    ci, ric, riy, riu, rid, cu, ruc, ruy, ruu, rud, own_i, own_u,
    load_sem, agi_s, agi_r, agu_s, agu_r,
    ici_s, ici_r, iy_s, iy_r, iz_s, iz_r,
    uci_s, uci_r, uy_s, uy_r, uz_s, uz_r,
):
    me = lax.axis_index("user")
    H = n // 4
    z = me // 4
    y = (me // 2) % 2
    c = me % 2
    oc = 1 - c
    oy = 1 - y
    K, T = uto.shape[1:]
    ub = unat.shape[0]
    ib = if_ref.shape[1] // T
    R = rat.shape[0]
    cap = w.shape[0] // n

    def at(zz, yy, cc):
        return zz * 4 + yy * 2 + cc

    core = at(z, y, oc)
    side = at(z, oy, c)
    up = at(z + 1, y, c)
    down = at(z - 1, y, c)
    has_up = z < H - 1
    has_down = z > 0

    def remote(src, dst, s, r, dev):
        return pltpu.make_async_remote_copy(
            src_ref=src, dst_ref=dst, send_sem=s, recv_sem=r,
            device_id={"user": dev}, device_id_type=pl.DeviceIdType.MESH,
        )

    loads = []
    parts = 4
    for q in range(parts):
        rows = pl.ds(q * (R // parts), R // parts)
        loads.append(pltpu.make_async_copy(rat_hbm.at[0, rows], rat.at[rows], load_sem.at[q]))
    for q in range(parts):
        rows = pl.ds(q * (n // parts), n // parts)
        wide = pl.ds(q * (n * cap // parts), n * cap // parts)
        loads.append(pltpu.make_async_copy(w_hbm.at[wide], w.at[wide], load_sem.at[parts + q]))

    for b in range(ib):
        t = if_ref[:, pl.ds(b * T, T)]
        itf[pl.ds(b * K, K), :] = t
        gi[me * ib + b] = t.astype(BF16)

    barrier = pltpu.get_barrier_semaphore()

    def greet(dev):
        pl.semaphore_signal(barrier, inc=1, device_id={"user": dev}, device_id_type=pl.DeviceIdType.MESH)

    greet(core)
    greet(side)

    @pl.when(has_up)
    def _():
        greet(up)

    @pl.when(has_down)
    def _():
        greet(down)

    pl.semaphore_wait(barrier, 2 + has_up.astype(jnp.int32) + has_down.astype(jnp.int32))

    class Gather:
        def __init__(self, buf, width, s, r):
            self.buf, self.width, self.s, self.r = buf, width, s, r

        def copy(self, o, way, dev):
            part = self.buf.at[pl.ds(o * self.width, self.width)]
            return remote(part, part, self.s.at[way, o], self.r.at[o], dev)

        def first(self):
            @pl.when(has_up)
            def _():
                self.copy(me, 0, up).start()

            @pl.when(has_down)
            def _():
                self.copy(me, 1, down).start()

            self.copy(me, 2, side).start()
            self.copy(me, 3, core).start()

        def from_side(self, zz):
            o = at(zz, oy, c)
            self.copy(o, 3, side).wait_recv()
            self.copy(o, 3, core).start()

        def step(self, t):
            @pl.when(z - t >= 0)
            def _():
                o = at(z - t, y, c)
                self.copy(o, 0, core).wait_recv()

                @pl.when(has_up)
                def _():
                    self.copy(o, 0, up).start()

                self.copy(o, 2, side).start()
                self.copy(o, 3, core).start()

            @pl.when(z + t < H)
            def _():
                o = at(z + t, y, c)
                self.copy(o, 1, core).wait_recv()

                @pl.when(has_down)
                def _():
                    self.copy(o, 1, down).start()

                self.copy(o, 2, side).start()
                self.copy(o, 3, core).start()

            self.late(t - 1)

        def late(self, t):
            @pl.when(z - t >= 0)
            def _():
                self.from_side(z - t)

            @pl.when(jnp.logical_and(z + t < H, t > 0))
            def _():
                self.from_side(z + t)

        def finish(self):
            self.late(H - 1)

            def arrive(k, _):
                o = at(k // 2, k % 2, oc)
                self.copy(o, 3, core).wait_recv()
                return 0

            lax.fori_loop(0, n // 2, arrive, 0)

        def drain(self):
            def sent(k, _):
                o = at(k, y, c)

                @pl.when(jnp.logical_and(has_up, k <= z))
                def _():
                    self.copy(o, 0, up).wait_send()

                @pl.when(jnp.logical_and(has_down, k >= z))
                def _():
                    self.copy(o, 1, down).wait_send()

                self.copy(o, 2, side).wait_send()
                self.copy(o, 3, core).wait_send()
                self.copy(at(k, oy, c), 3, core).wait_send()
                return 0

            lax.fori_loop(0, H, sent, 0)

    items = Gather(gi, ib, agi_s, agi_r)
    users = Gather(gu, ub, agu_s, agu_r)
    items.first()
    for load in loads:
        load.start()

    zero = jnp.zeros((K, T), BF16)
    for b in range(ub):
        t = uf_ref[:, pl.ds(b * T, T)]
        unat[b] = jnp.transpose(t).astype(BF16)
        utf[pl.ds(b * K, K), :] = t
        t = t.astype(BF16)
        gu[me * ub + b] = t
        uto[b] = t
    gi[n * ib] = zero
    scaled[ub] = zero
    items.step(1)
    users.first()
    lent = jnp.transpose(len_ref[0].astype(F32))
    for g in range(R // GROUP):
        lens[g] = lent[:, g * GROUP:(g + 1) * GROUP]
    run[0] = jnp.zeros((K, T), F32)
    uacc[...] = jnp.zeros(uacc.shape, F32)
    pacc[...] = jnp.zeros(pacc.shape, F32)
    for t in range(2, H):
        items.step(t)
    items.finish()
    for load in loads[:parts]:
        load.wait()

    columns = lax.broadcasted_iota(jnp.int32, (T, T), 1).astype(F32)
    every = (R // GROUP) // H

    def rate(g, _):
        @pl.when(jnp.logical_and(g % every == 0, g // every + 1 < H))
        def _():
            users.step(g // every + 1)

        cut = lens[g]
        errs = []
        picks = []
        for j in range(GROUP):
            r = g * GROUP + j
            u = ruser[0, r]
            i = ritem[0, r]
            pred = jnp.dot(unat[u], gi[i], preferred_element_type=F32)
            e = jnp.where(columns < cut[:, j:j + 1], pred - rat[r].astype(F32), 0.0).astype(BF16)
            errs.append(e)
            picks.append(jnp.concatenate(
                [gi[jnp.where(u == b, i, n * ib)] for b in range(ub)], axis=0))
            term = jnp.dot(uto[u], e, preferred_element_type=F32)
            run[r + 1] = term + run[links[r]]
        uacc[...] += lax.dot_general(
            jnp.concatenate(picks, axis=1), jnp.concatenate(errs, axis=1), NT,
            preferred_element_type=F32)
        return 0

    lax.fori_loop(0, R // GROUP, rate, 0)

    class Reduce:
        def __init__(self, buf, width, rc, ry, ru, rd, own, cs, cr, ys, yr, zs, zr):
            self.buf, self.width, self.own = buf, width, own
            self.rc, self.ry, self.ru, self.rd = rc, ry, ru, rd
            self.cs, self.cr, self.ys, self.yr, self.zs, self.zr = cs, cr, ys, yr, zs, zr

        def cross(self, zz, yy):
            k = zz * 2 + yy
            return remote(self.buf.at[at(zz, yy, oc)], self.rc.at[k], self.cs.at[k], self.cr.at[k], core)

        def aside(self, zz):
            return remote(self.buf.at[at(zz, oy, c)], self.ry.at[zz], self.ys.at[zz], self.yr.at[zz], side)

        def climb(self, zz):
            return remote(self.buf.at[at(zz, y, c)], self.ru.at[zz], self.zs.at[zz], self.zr.at[0, zz], up)

        def sink(self, zz):
            return remote(self.buf.at[at(zz, y, c)], self.rd.at[zz], self.zs.at[zz], self.zr.at[1, zz], down)

        def turn(self, zz):
            self.cross(zz, oy).wait_recv()
            d = at(zz, oy, c)
            self.buf[d] = (self.buf[d].astype(F32) + self.rc[zz * 2 + oy].astype(F32)).astype(BF16)
            self.aside(zz).start()

        def line(self, zz):
            d = at(zz, y, c)
            self.cross(zz, y).wait_recv()
            self.aside(zz).wait_recv()
            self.own[...] = (self.buf[d].astype(F32) + self.rc[zz * 2 + y].astype(F32)
                             + self.ry[zz].astype(F32))

            @pl.when(jnp.logical_and(z <= zz, has_down))
            def _():
                self.climb(zz).wait_recv()
                self.own[...] += self.ru[zz].astype(F32)

            @pl.when(jnp.logical_and(z >= zz, has_up))
            def _():
                self.sink(zz).wait_recv()
                self.own[...] += self.rd[zz].astype(F32)

            @pl.when(z != zz)
            def _():
                self.buf[d] = self.own[...].astype(BF16)

            @pl.when(z < zz)
            def _():
                self.climb(zz).start()

            @pl.when(z > zz)
            def _():
                self.sink(zz).start()

            @pl.when(z == zz)
            def _():
                self.buf_own[...] = self.own[...]

        def drain(self):
            def sent(k, _):
                self.cross(k, 0).wait_send()
                self.cross(k, 1).wait_send()
                self.aside(k).wait_send()

                @pl.when(z < k)
                def _():
                    self.climb(k).wait_send()

                @pl.when(z > k)
                def _():
                    self.sink(k).wait_send()

                return 0

            lax.fori_loop(0, H, sent, 0)

    item_sum = Reduce(ci, ib, ric, riy, riu, rid, own_i.at[0], ici_s, ici_r, iy_s, iy_r, iz_s, iz_r)
    item_sum.buf_own = own_i.at[1]
    user_sum = Reduce(cu, ub, ruc, ruy, ruu, rud, own_u.at[0], uci_s, uci_r, uy_s, uy_r, uz_s, uz_r)
    user_sum.buf_own = own_u.at[1]

    low = (2 * z < H).astype(jnp.int32)

    def order(k):
        last = (k == H - 1).astype(jnp.int32)
        near = (k < H - 1 - z).astype(jnp.int32)
        far = (k < z).astype(jnp.int32)
        rising = near * (H - 1 - k) + (1 - near) * (k - (H - 1 - z))
        falling = far * k + (1 - far) * (H - 1 - (k - z))
        return last * z + (1 - last) * (low * rising + (1 - low) * falling)

    def fill(d):
        for b in range(ib):
            ci[d, pl.ds(b * K, K), :] = run[links[R + d * ib + b]].astype(BF16)

    def fill_other(k, _):
        for yy in (oy, y):
            fill(at(order(k), yy, oc))
            item_sum.cross(order(k), yy).start()
        return 0

    def fill_mine(k, _):
        for yy in (oy, y):
            fill(at(order(k), yy, c))
        return 0

    lax.fori_loop(0, H, fill_other, 0)
    lax.fori_loop(0, H, fill_mine, 0)
    users.finish()
    gu[n * ub] = zero
    for load in loads[parts:]:
        load.wait()

    row = lax.broadcasted_iota(jnp.int32, (16, T), 0)

    def pull(p, _):
        @pl.when(jnp.logical_and(p >= n - H, p < n))
        def _():
            item_sum.turn(order(p - (n - H)))

        lhs = []
        rhs = []
        for k in range(cap):
            s = tsrc[k, 0, p]
            t = p * ub + tdst[k, 0, p]
            ones = jnp.where(row == s, 1.0, 0.0).astype(BF16)
            lhs.append(jnp.concatenate(
                [gu[jnp.where(s == b, t, n * ub)] for b in range(ub)] + [ones], axis=0))
            rhs.append(w[p * cap + k])
        pacc[...] += lax.dot_general(
            jnp.concatenate(lhs, axis=1), jnp.concatenate(rhs, axis=1), NT,
            preferred_element_type=F32)
        return 0

    lax.fori_loop(0, n, pull, 0)
    for b in range(ub):
        den = 1.0 + pacc[ub * K + b:ub * K + b + 1, :]
        rows = pl.ds(b * K, K)
        err = utf[rows, :] - pacc[rows, :] / den
        pe[rows, :] = err
        scaled[b] = (err / den).astype(BF16)

    def give(p):
        lhs = []
        for k in range(cap):
            s = tsrc[k, 0, p]
            t = tdst[k, 0, p]
            lhs.append(jnp.concatenate(
                [scaled[jnp.where(t == b, s, ub)] for b in range(ub)], axis=0))
        tiles = w[pl.ds(p * cap, cap)].reshape(cap * T, T)
        cu[p] = jnp.dot(jnp.concatenate(lhs, axis=1), tiles, preferred_element_type=F32).astype(BF16)

    def give_other(k, _):
        zz = order(k % H)
        yy = (k // H) * y + (1 - k // H) * oy
        give(at(zz, yy, oc))
        user_sum.cross(zz, yy).start()
        return 0

    def give_side(k, _):
        zz = order(k)
        give(at(zz, oy, c))
        user_sum.turn(zz)
        return 0

    def give_mine(k, _):
        give(at(order(k), y, c))
        item_sum.line(order(k))
        return 0

    def user_line(k, _):
        user_sum.line(order(k))
        return 0

    lax.fori_loop(0, 2 * H, give_other, 0)
    lax.fori_loop(0, H, give_side, 0)
    lax.fori_loop(0, H, give_mine, 0)
    for b in range(ib):
        rows = pl.ds(b * K, K)
        ig_ref[:, pl.ds(b * T, T)] = own_i[1, rows, :] + reg_coef * itf[rows, :]
    lax.fori_loop(0, H, user_line, 0)
    for b in range(ub):
        rows = pl.ds(b * K, K)
        total = (uacc[rows, :] + social_coef * (pe[rows, :] - own_u[1, rows, :])
                 + reg_coef * utf[rows, :])
        ug_ref[:, pl.ds(b * T, T)] = total
    items.drain()
    users.drain()
    item_sum.drain()
    user_sum.drain()


def body(n, user_factors, item_factors, ratings, rating_len, rating_user, rating_item,
         trust_src, trust_dst, trust_weight):
    T = ratings.shape[-1]
    K = user_factors.shape[1]
    ub = user_factors.shape[0] // T
    ib = item_factors.shape[0] // T
    R = ratings.shape[1]
    cap = trust_src.shape[2]
    H = n // 4
    tile_items = rating_item[0]
    ids = jnp.concatenate([tile_items, jnp.arange(n * ib, dtype=jnp.int32)])
    limit = jnp.minimum(jnp.arange(R + n * ib, dtype=jnp.int32), R)
    at = jnp.arange(R, dtype=jnp.int32)
    links = jnp.max(jnp.where((ids[:, None] == tile_items[None, :]) & (at[None, :] < limit[:, None]),
                              at[None, :] + 1, 0), axis=1)
    weights = trust_weight.reshape(n * cap, T, T)
    vmem = pl.BlockSpec(memory_space=pltpu.VMEM)
    smem = pl.BlockSpec(memory_space=pltpu.SMEM)
    hbm = pl.BlockSpec(memory_space=pl.ANY)
    dma = pltpu.SemaphoreType.DMA
    scratch = [
        pltpu.VMEM((R, T, T), BF16),
        pltpu.VMEM((n * cap, T, T), BF16),
        pltpu.VMEM((n * ib + 1, K, T), BF16),
        pltpu.VMEM((n * ub + 1, K, T), BF16),
        pltpu.VMEM((ub, T, K), BF16),
        pltpu.VMEM((ub * K, T), F32),
        pltpu.VMEM((ib * K, T), F32),
        pltpu.VMEM((ub, K, T), BF16),
        pltpu.VMEM((R // GROUP, T, GROUP), F32),
        pltpu.VMEM((R + 1, K, T), F32),
        pltpu.VMEM((ub * K, T), F32),
        pltpu.VMEM((ub * K + 16, T), F32),
        pltpu.VMEM((ub * K, T), F32),
        pltpu.VMEM((ub + 1, K, T), BF16),
    ]
    for width in (ib, ub):
        scratch += [pltpu.VMEM((count, width * K, T), BF16) for count in (n, n // 2, H, H, H)]
    scratch += [pltpu.VMEM((2, width * K, T), F32) for width in (ib, ub)]
    scratch += [dma((8,)), dma((4, n)), dma((n,)), dma((4, n)), dma((n,))]
    for _ in range(2):
        scratch += [dma((n // 2,)), dma((n // 2,)), dma((H,)), dma((H,)), dma((H,)), dma((2, H))]
    user_grad, item_grad = pl.pallas_call(
        functools.partial(kernel, n),
        out_shape=(jax.ShapeDtypeStruct((K, ub * T), F32),
                   jax.ShapeDtypeStruct((K, ib * T), F32)),
        in_specs=[vmem, vmem, hbm, vmem, smem, smem, smem, smem, hbm, smem],
        out_specs=(vmem, vmem),
        scratch_shapes=scratch,
        compiler_params=pltpu.CompilerParams(
            collective_id=0, has_side_effects=True, vmem_limit_bytes=56 * 1024 * 1024),
    )(user_factors.T, item_factors.T, ratings, rating_len, rating_user, rating_item,
      trust_src.transpose(2, 0, 1), trust_dst.transpose(2, 0, 1), weights, links)
    return user_grad.T, item_grad.T


def solution(mesh):
    row = P(("parts", "user"))
    return jax.shard_map(
        functools.partial(body, mesh.shape["user"]), mesh=mesh,
        in_specs=(row,) * 9, out_specs=(row, row), check_vma=False)
```

```python
import functools

import jax
import jax.numpy as jnp
from jax import lax
from jax.experimental import pallas as pl
from jax.experimental.pallas import tpu as pltpu
from jax.sharding import PartitionSpec as P

reg_coef = 0.05
social_coef = 8.0
GROUP = 4
NT = (((1,), (1,)), ((), ()))
F32 = jnp.float32
BF16 = jnp.bfloat16


def kernel(
    n, uf_ref, if_ref, rat_hbm, len_ref, ruser, ritem, tsrc, tdst, w_hbm, links,
    ug_ref, ig_ref,
    rat, w, gi, gu, unat, utf, itf, uto, lens, run, uacc, pacc, pe, scaled, held,
    ci, ric, riy, riu, rid, cu, ruc, ruy, ruu, rud, own_i, own_u,
    load_sem, agi_s, agi_r, agu_s, agu_r,
    ici_s, ici_r, iy_s, iy_r, iz_s, iz_r,
    uci_s, uci_r, uy_s, uy_r, uz_s, uz_r,
):
    me = lax.axis_index("user")
    H = n // 4
    z = me // 4
    y = (me // 2) % 2
    c = me % 2
    oc = 1 - c
    oy = 1 - y
    K, T = uto.shape[1:]
    ub = unat.shape[0]
    ib = if_ref.shape[1] // T
    R = rat.shape[0]
    cap = w.shape[0] // n

    def at(zz, yy, cc):
        return zz * 4 + yy * 2 + cc

    core = at(z, y, oc)
    side = at(z, oy, c)
    up = at(z + 1, y, c)
    down = at(z - 1, y, c)
    has_up = z < H - 1
    has_down = z > 0

    def remote(src, dst, s, r, dev):
        return pltpu.make_async_remote_copy(
            src_ref=src, dst_ref=dst, send_sem=s, recv_sem=r,
            device_id={"user": dev}, device_id_type=pl.DeviceIdType.MESH,
        )

    loads = []
    parts = 4
    for q in range(parts):
        rows = pl.ds(q * (R // parts), R // parts)
        loads.append(pltpu.make_async_copy(rat_hbm.at[0, rows], rat.at[rows], load_sem.at[q]))
    for q in range(parts):
        rows = pl.ds(q * (n // parts), n // parts)
        wide = pl.ds(q * (n * cap // parts), n * cap // parts)
        loads.append(pltpu.make_async_copy(w_hbm.at[wide], w.at[wide], load_sem.at[parts + q]))

    for b in range(ib):
        t = if_ref[:, pl.ds(b * T, T)]
        itf[pl.ds(b * K, K), :] = t
        gi[me * ib + b] = t.astype(BF16)

    barrier = pltpu.get_barrier_semaphore()

    def greet(dev):
        pl.semaphore_signal(barrier, inc=1, device_id={"user": dev}, device_id_type=pl.DeviceIdType.MESH)

    greet(core)
    greet(side)

    @pl.when(has_up)
    def _():
        greet(up)

    @pl.when(has_down)
    def _():
        greet(down)

    pl.semaphore_wait(barrier, 2 + has_up.astype(jnp.int32) + has_down.astype(jnp.int32))

    class Gather:
        def __init__(self, buf, width, s, r):
            self.buf, self.width, self.s, self.r = buf, width, s, r

        def copy(self, o, way, dev):
            part = self.buf.at[pl.ds(o * self.width, self.width)]
            return remote(part, part, self.s.at[way, o], self.r.at[o], dev)

        def first(self):
            @pl.when(has_up)
            def _():
                self.copy(me, 0, up).start()

            @pl.when(has_down)
            def _():
                self.copy(me, 1, down).start()

            self.copy(me, 2, side).start()
            self.copy(me, 3, core).start()

        def from_side(self, zz):
            o = at(zz, oy, c)
            self.copy(o, 3, side).wait_recv()
            self.copy(o, 3, core).start()

        def step(self, t):
            @pl.when(z - t >= 0)
            def _():
                o = at(z - t, y, c)
                self.copy(o, 0, core).wait_recv()

                @pl.when(has_up)
                def _():
                    self.copy(o, 0, up).start()

                self.copy(o, 2, side).start()
                self.copy(o, 3, core).start()

            @pl.when(z + t < H)
            def _():
                o = at(z + t, y, c)
                self.copy(o, 1, core).wait_recv()

                @pl.when(has_down)
                def _():
                    self.copy(o, 1, down).start()

                self.copy(o, 2, side).start()
                self.copy(o, 3, core).start()

            self.late(t - 1)

        def late(self, t):
            @pl.when(z - t >= 0)
            def _():
                self.from_side(z - t)

            @pl.when(jnp.logical_and(z + t < H, t > 0))
            def _():
                self.from_side(z + t)

        def finish(self):
            self.late(H - 1)

            def arrive(k, _):
                o = at(k // 2, k % 2, oc)
                self.copy(o, 3, core).wait_recv()
                return 0

            lax.fori_loop(0, n // 2, arrive, 0)

        def drain(self):
            def sent(k, _):
                o = at(k, y, c)

                @pl.when(jnp.logical_and(has_up, k <= z))
                def _():
                    self.copy(o, 0, up).wait_send()

                @pl.when(jnp.logical_and(has_down, k >= z))
                def _():
                    self.copy(o, 1, down).wait_send()

                self.copy(o, 2, side).wait_send()
                self.copy(o, 3, core).wait_send()
                self.copy(at(k, oy, c), 3, core).wait_send()
                return 0

            lax.fori_loop(0, H, sent, 0)

    items = Gather(gi, ib, agi_s, agi_r)
    users = Gather(gu, ub, agu_s, agu_r)
    items.first()
    for load in loads:
        load.start()

    zero = jnp.zeros((K, T), BF16)
    for b in range(ub):
        t = uf_ref[:, pl.ds(b * T, T)]
        unat[b] = jnp.transpose(t).astype(BF16)
        utf[pl.ds(b * K, K), :] = t
        t = t.astype(BF16)
        gu[me * ub + b] = t
        uto[b] = t
    gi[n * ib] = zero
    scaled[ub] = zero
    items.step(1)
    users.first()
    lent = jnp.transpose(len_ref[0].astype(F32))
    for g in range(R // GROUP):
        lens[g] = lent[:, g * GROUP:(g + 1) * GROUP]
    run[0] = jnp.zeros((K, T), F32)
    uacc[...] = jnp.zeros(uacc.shape, F32)
    pacc[...] = jnp.zeros(pacc.shape, F32)
    for t in range(2, H):
        items.step(t)
    items.finish()
    for load in loads[:parts]:
        load.wait()

    columns = lax.broadcasted_iota(jnp.int32, (T, T), 1).astype(F32)
    every = (R // GROUP) // H

    def predict(g):
        cut = lens[g]
        errs = []
        for j in range(GROUP):
            r = g * GROUP + j
            pred = jnp.dot(unat[ruser[0, r]], gi[ritem[0, r]], preferred_element_type=F32)
            errs.append(jnp.where(
                columns < cut[:, j:j + 1], pred - rat[r].astype(F32), 0.0).astype(BF16))
        return errs

    def spread(g, errs):
        picks = []
        terms = []
        for j in range(GROUP):
            r = g * GROUP + j
            u = ruser[0, r]
            i = ritem[0, r]
            picks.append(jnp.concatenate(
                [gi[jnp.where(u == b, i, n * ib)] for b in range(ub)], axis=0))
            terms.append(jnp.dot(uto[u], errs[j], preferred_element_type=F32))
        uacc[...] += lax.dot_general(
            jnp.concatenate(picks, axis=1), jnp.concatenate(errs, axis=1), NT,
            preferred_element_type=F32)
        for j in range(GROUP):
            r = g * GROUP + j
            run[r + 1] = terms[j] + run[links[r]]

    def travel(g):
        @pl.when(jnp.logical_and(g % every == 0, g // every + 1 < H))
        def _():
            users.step(g // every + 1)

    def keep(g):
        for j, e in enumerate(predict(g)):
            held[j] = e

    def rate(g, _):
        travel(g)
        spread(g - 1, [held[j] for j in range(GROUP)])
        keep(g)
        return 0

    travel(0)
    keep(0)
    lax.fori_loop(1, R // GROUP, rate, 0)
    spread(R // GROUP - 1, [held[j] for j in range(GROUP)])

    class Reduce:
        def __init__(self, buf, width, rc, ry, ru, rd, own, cs, cr, ys, yr, zs, zr):
            self.buf, self.width, self.own = buf, width, own
            self.rc, self.ry, self.ru, self.rd = rc, ry, ru, rd
            self.cs, self.cr, self.ys, self.yr, self.zs, self.zr = cs, cr, ys, yr, zs, zr

        def cross(self, zz, yy):
            k = zz * 2 + yy
            return remote(self.buf.at[at(zz, yy, oc)], self.rc.at[k], self.cs.at[k], self.cr.at[k], core)

        def aside(self, zz):
            return remote(self.buf.at[at(zz, oy, c)], self.ry.at[zz], self.ys.at[zz], self.yr.at[zz], side)

        def climb(self, zz):
            return remote(self.buf.at[at(zz, y, c)], self.ru.at[zz], self.zs.at[zz], self.zr.at[0, zz], up)

        def sink(self, zz):
            return remote(self.buf.at[at(zz, y, c)], self.rd.at[zz], self.zs.at[zz], self.zr.at[1, zz], down)

        def turn(self, zz):
            self.cross(zz, oy).wait_recv()
            d = at(zz, oy, c)
            self.buf[d] = (self.buf[d].astype(F32) + self.rc[zz * 2 + oy].astype(F32)).astype(BF16)
            self.aside(zz).start()

        def line(self, zz):
            d = at(zz, y, c)
            self.cross(zz, y).wait_recv()
            self.aside(zz).wait_recv()
            self.own[...] = (self.buf[d].astype(F32) + self.rc[zz * 2 + y].astype(F32)
                             + self.ry[zz].astype(F32))

            @pl.when(jnp.logical_and(z <= zz, has_down))
            def _():
                self.climb(zz).wait_recv()
                self.own[...] += self.ru[zz].astype(F32)

            @pl.when(jnp.logical_and(z >= zz, has_up))
            def _():
                self.sink(zz).wait_recv()
                self.own[...] += self.rd[zz].astype(F32)

            @pl.when(z != zz)
            def _():
                self.buf[d] = self.own[...].astype(BF16)

            @pl.when(z < zz)
            def _():
                self.climb(zz).start()

            @pl.when(z > zz)
            def _():
                self.sink(zz).start()

            @pl.when(z == zz)
            def _():
                self.buf_own[...] = self.own[...]

        def drain(self):
            def sent(k, _):
                self.cross(k, 0).wait_send()
                self.cross(k, 1).wait_send()
                self.aside(k).wait_send()

                @pl.when(z < k)
                def _():
                    self.climb(k).wait_send()

                @pl.when(z > k)
                def _():
                    self.sink(k).wait_send()

                return 0

            lax.fori_loop(0, H, sent, 0)

    item_sum = Reduce(ci, ib, ric, riy, riu, rid, own_i.at[0], ici_s, ici_r, iy_s, iy_r, iz_s, iz_r)
    item_sum.buf_own = own_i.at[1]
    user_sum = Reduce(cu, ub, ruc, ruy, ruu, rud, own_u.at[0], uci_s, uci_r, uy_s, uy_r, uz_s, uz_r)
    user_sum.buf_own = own_u.at[1]

    low = (2 * z < H).astype(jnp.int32)

    def order(k):
        last = (k == H - 1).astype(jnp.int32)
        near = (k < H - 1 - z).astype(jnp.int32)
        far = (k < z).astype(jnp.int32)
        rising = near * (H - 1 - k) + (1 - near) * (k - (H - 1 - z))
        falling = far * k + (1 - far) * (H - 1 - (k - z))
        return last * z + (1 - last) * (low * rising + (1 - low) * falling)

    def fill(d):
        for b in range(ib):
            ci[d, pl.ds(b * K, K), :] = run[links[R + d * ib + b]].astype(BF16)

    def fill_other(k, _):
        for yy in (oy, y):
            fill(at(order(k), yy, oc))
            item_sum.cross(order(k), yy).start()
        return 0

    def fill_mine(k, _):
        fill(at(order(k), oy, c))
        item_sum.turn(order(k))
        fill(at(order(k), y, c))
        return 0

    lax.fori_loop(0, H, fill_other, 0)
    lax.fori_loop(0, H, fill_mine, 0)
    users.finish()
    gu[n * ub] = zero
    for load in loads[parts:]:
        load.wait()

    row = lax.broadcasted_iota(jnp.int32, (16, T), 0)

    def pull(p, _):
        @pl.when(p > n - H)
        def _():
            item_sum.line(order(p - (n - H) - 1))

        lhs = []
        rhs = []
        for k in range(cap):
            s = tsrc[k, 0, p]
            t = p * ub + tdst[k, 0, p]
            ones = jnp.where(row == s, 1.0, 0.0).astype(BF16)
            lhs.append(jnp.concatenate(
                [gu[jnp.where(s == b, t, n * ub)] for b in range(ub)] + [ones], axis=0))
            rhs.append(w[p * cap + k])
        pacc[...] += lax.dot_general(
            jnp.concatenate(lhs, axis=1), jnp.concatenate(rhs, axis=1), NT,
            preferred_element_type=F32)
        return 0

    lax.fori_loop(0, n, pull, 0)
    for b in range(ub):
        den = 1.0 + pacc[ub * K + b:ub * K + b + 1, :]
        rows = pl.ds(b * K, K)
        err = utf[rows, :] - pacc[rows, :] / den
        pe[rows, :] = err
        scaled[b] = (err / den).astype(BF16)

    def give(p):
        lhs = []
        for k in range(cap):
            s = tsrc[k, 0, p]
            t = tdst[k, 0, p]
            lhs.append(jnp.concatenate(
                [scaled[jnp.where(t == b, s, ub)] for b in range(ub)], axis=0))
        tiles = w[pl.ds(p * cap, cap)].reshape(cap * T, T)
        cu[p] = jnp.dot(jnp.concatenate(lhs, axis=1), tiles, preferred_element_type=F32).astype(BF16)

    def give_across(k, yy):
        zz = order(k)
        give(at(zz, yy, oc))
        user_sum.cross(zz, yy).start()
        return yy

    def give_side(k, _):
        zz = order(k)
        give(at(zz, oy, c))
        user_sum.turn(zz)
        return 0

    def give_mine(k, _):
        give(at(order(k), y, c))
        return 0

    def user_line(k, _):
        user_sum.line(order(k))
        return 0

    lax.fori_loop(0, H, give_across, oy)
    lax.fori_loop(0, H, give_side, 0)
    lax.fori_loop(0, H, give_across, y)
    lax.fori_loop(0, H, give_mine, 0)
    item_sum.line(z)
    for b in range(ib):
        rows = pl.ds(b * K, K)
        ig_ref[:, pl.ds(b * T, T)] = own_i[1, rows, :] + reg_coef * itf[rows, :]
    lax.fori_loop(0, H, user_line, 0)
    for b in range(ub):
        rows = pl.ds(b * K, K)
        total = (uacc[rows, :] + social_coef * (pe[rows, :] - own_u[1, rows, :])
                 + reg_coef * utf[rows, :])
        ug_ref[:, pl.ds(b * T, T)] = total
    items.drain()
    users.drain()
    item_sum.drain()
    user_sum.drain()


def body(n, user_factors, item_factors, ratings, rating_len, rating_user, rating_item,
         trust_src, trust_dst, trust_weight):
    T = ratings.shape[-1]
    K = user_factors.shape[1]
    ub = user_factors.shape[0] // T
    ib = item_factors.shape[0] // T
    R = ratings.shape[1]
    cap = trust_src.shape[2]
    H = n // 4
    tile_items = rating_item[0]
    ids = jnp.concatenate([tile_items, jnp.arange(n * ib, dtype=jnp.int32)])
    limit = jnp.minimum(jnp.arange(R + n * ib, dtype=jnp.int32), R)
    at = jnp.arange(R, dtype=jnp.int32)
    links = jnp.max(jnp.where((ids[:, None] == tile_items[None, :]) & (at[None, :] < limit[:, None]),
                              at[None, :] + 1, 0), axis=1)
    weights = trust_weight.reshape(n * cap, T, T)
    vmem = pl.BlockSpec(memory_space=pltpu.VMEM)
    smem = pl.BlockSpec(memory_space=pltpu.SMEM)
    hbm = pl.BlockSpec(memory_space=pl.ANY)
    dma = pltpu.SemaphoreType.DMA
    scratch = [
        pltpu.VMEM((R, T, T), BF16),
        pltpu.VMEM((n * cap, T, T), BF16),
        pltpu.VMEM((n * ib + 1, K, T), BF16),
        pltpu.VMEM((n * ub + 1, K, T), BF16),
        pltpu.VMEM((ub, T, K), BF16),
        pltpu.VMEM((ub * K, T), F32),
        pltpu.VMEM((ib * K, T), F32),
        pltpu.VMEM((ub, K, T), BF16),
        pltpu.VMEM((R // GROUP, T, GROUP), F32),
        pltpu.VMEM((R + 1, K, T), F32),
        pltpu.VMEM((ub * K, T), F32),
        pltpu.VMEM((ub * K + 16, T), F32),
        pltpu.VMEM((ub * K, T), F32),
        pltpu.VMEM((ub + 1, K, T), BF16),
        pltpu.VMEM((GROUP, T, T), BF16),
    ]
    for width in (ib, ub):
        scratch += [pltpu.VMEM((count, width * K, T), BF16) for count in (n, n // 2, H, H, H)]
    scratch += [pltpu.VMEM((2, width * K, T), F32) for width in (ib, ub)]
    scratch += [dma((8,)), dma((4, n)), dma((n,)), dma((4, n)), dma((n,))]
    for _ in range(2):
        scratch += [dma((n // 2,)), dma((n // 2,)), dma((H,)), dma((H,)), dma((H,)), dma((2, H))]
    user_grad, item_grad = pl.pallas_call(
        functools.partial(kernel, n),
        out_shape=(jax.ShapeDtypeStruct((K, ub * T), F32),
                   jax.ShapeDtypeStruct((K, ib * T), F32)),
        in_specs=[vmem, vmem, hbm, vmem, smem, smem, smem, smem, hbm, smem],
        out_specs=(vmem, vmem),
        scratch_shapes=scratch,
        compiler_params=pltpu.CompilerParams(
            collective_id=0, has_side_effects=True, vmem_limit_bytes=56 * 1024 * 1024),
    )(user_factors.T, item_factors.T, ratings, rating_len, rating_user, rating_item,
      trust_src.transpose(2, 0, 1), trust_dst.transpose(2, 0, 1), weights, links)
    return user_grad.T, item_grad.T


def solution(mesh):
    row = P(("parts", "user"))
    return jax.shard_map(
        functools.partial(body, mesh.shape["user"]), mesh=mesh,
        in_specs=(row,) * 9, out_specs=(row, row), check_vma=False)
```
